32 devices in a mesh: groups: 2 (over y), blk: 4 (over z), feat: 4 (over x, core).
Axes of the slice: x: 2, y: 2, z: 4, core: 2. Of those that a mesh axis runs over, the one named last changes fastest.
Arguments:
- queries: bfloat16 [512, 16384], P(('groups', 'blk'), 'feat'), parts along dimension 0, may hold values from -6 to 6
- train_grads: bfloat16 [4096, 16384], P(('groups', 'blk'), 'feat'), parts along dimension 0, may hold values from -6 to 6
- precond: float32 [16384], P('feat'), may hold values from 0.3 to 27
- counts: int32 [8], P(('groups', 'blk')), parts along dimension 0, may hold values from 128 to 512, as said below
- segment_ids: int32 [512], P('groups'), parts along dimension 0, may hold values from 0 to 127, as said below
- flagged: int32 [128], P('groups'), parts along dimension 0, may hold values from 0 to 127, as said below
Outputs:
- attribution: float32 [4096, 64], P(('groups', 'blk', 'feat')), parts along dimension 0
The draws below stay inside these ranges and needn't reach their ends.
There are 2 independent parts, one for each index of `groups`. The reference program is written for one: setup_inputs(seed, part) draws one part's arguments, and reference() takes and returns one part's arrays. A program takes and returns all parts, laid end to end along the dimension named above; an argument that names none is the same for every part. Nothing has to cross between parts.
Inputs may be any that keep to these rules, and one draw needn't show every extreme that they name: counts[k] is the number of live rows of shard k; one shard is full. `segment_ids`: segment ids never fall; every segment of 0 to 127 holds at least one row; each block of 64 consecutive query rows holds exactly 32 rows of flagged segments. `flagged`: distinct segments; together they hold exactly 128 query rows.
All inputs are finite; a program needn't handle non-finite values.
Results may differ from the reference program's by a relative error of at most 0.0028.
Values may be sent and summed in bfloat16 or wider, within the bound.
A program may use at most 64 MiB of HBM per device.

```python
import math
import jax
import jax.numpy as jnp
from jax import lax

F = 16384
QDEV = 64
TDEV = 512
LABELS = 64
Q = 256
NTRAIN = 2048
N_BLK = 4


def split_lengths(key, total, parts):
    extra = total - parts
    picks = jax.random.randint(key, (N_BLK, extra), 0, parts).astype(jnp.int32)
    hits = (picks[:, :, None] == jnp.arange(parts, dtype=jnp.int32)[None, None, :]).astype(jnp.int32)
    return (jnp.sum(hits, axis=1) + 1).astype(jnp.int32)


def segment_plan(key):
    per_shard = LABELS // N_BLK
    half = QDEV // 2
    shard_keys = jax.random.split(jax.random.fold_in(key, 201), N_BLK)
    orders = jax.vmap(lambda one: jax.random.permutation(one, 2 * per_shard))(shard_keys).astype(jnp.int32)
    flag_lengths = split_lengths(jax.random.fold_in(key, 202), half, per_shard)
    other_lengths = split_lengths(jax.random.fold_in(key, 203), QDEV - half, per_shard)
    shard_index = jnp.broadcast_to(jnp.arange(N_BLK, dtype=jnp.int32)[:, None], (N_BLK, 2 * per_shard))
    lengths = jnp.zeros((N_BLK, 2 * per_shard), jnp.int32).at[shard_index, orders].set(jnp.concatenate([flag_lengths, other_lengths], axis=1))
    chosen = (jnp.arange(N_BLK, dtype=jnp.int32)[:, None] * (2 * per_shard) + orders[:, :per_shard]).reshape(LABELS)
    shuffle = jax.random.permutation(jax.random.fold_in(key, 204), LABELS).astype(jnp.int32)
    return (lengths, chosen[shuffle].astype(jnp.int32))


def draw_flagged(key, part):
    lengths, chosen = segment_plan(key)
    return chosen.astype(jnp.int32)


def draw_segment_ids(key, part):
    lengths, chosen = segment_plan(key)
    per_shard = LABELS // N_BLK
    ends = jnp.cumsum(lengths, axis=1)
    positions = jnp.arange(QDEV, dtype=jnp.int32)
    local = jnp.sum((ends[:, None, :] <= positions[None, :, None]).astype(jnp.int32), axis=2)
    result = jnp.arange(N_BLK, dtype=jnp.int32)[:, None] * (2 * per_shard) + local
    return result.reshape(Q).astype(jnp.int32)


def draw_counts(key, part):
    key = jax.random.fold_in(key, 5)
    values = jax.random.randint(key, (N_BLK,), TDEV // 4, TDEV + 1).astype(jnp.int32)
    fullest = jax.random.randint(jax.random.fold_in(key, 11), (), 0, N_BLK)
    return values.at[fullest].set(TDEV).astype(jnp.int32)


def draw_precond(key, part):
    key = jax.random.fold_in(key, 7)
    positions = jnp.arange(F, dtype=jnp.float32) / F
    base = jnp.exp(jax.random.uniform(key, (F,), jnp.float32, jnp.log(0.3), jnp.log(3.0)))
    rising = jnp.exp(jnp.log(3.0) * positions)
    return (base * rising).astype(jnp.float32)


def steps_of(rng, dims, pieces, least, largest):
    loudness, own = 1.0, jax.random.fold_in(rng, 6)
    for position, blocks in pieces:
        steps = jnp.exp(jax.random.uniform(jax.random.fold_in(own, position), (blocks,), jnp.float32, least / len(pieces), largest / len(pieces)))
        loudness = loudness * jnp.repeat(steps, dims[position] // blocks).reshape([-1 if axis == position else 1 for axis in range(len(dims))])
    return loudness


def gaussian(rng, shape, spread, most, cuts=(), held_as=jnp.bfloat16):
    loudness = steps_of(rng, shape, cuts, -0.22, 0.18) if cuts else 1.0
    values = jax.random.normal(rng, shape, jnp.float32) * spread * loudness
    return jnp.minimum(jnp.maximum(values, -most), most).astype(held_as)


def setup_inputs(seed: int = 0, part: int = 0) -> dict:
    keys = jax.random.split(jax.random.key(seed), 7)
    part_splits = jax.random.split(jax.random.fold_in(keys[6], part), 7)
    return {
        "queries": gaussian(part_splits[0], (Q, F), 1.0, 6.0, ((0, 4), (1, 4))),
        "train_grads": gaussian(part_splits[1], (NTRAIN, F), 1.0, 6.0, ((0, 4), (1, 4))),
        "precond": draw_precond(jax.random.fold_in(keys[6], 71), part),
        "counts": draw_counts(jax.random.fold_in(jax.random.fold_in(keys[6], part), 71), part),
        "segment_ids": draw_segment_ids(jax.random.fold_in(jax.random.fold_in(keys[6], part), 71), part),
        "flagged": draw_flagged(jax.random.fold_in(jax.random.fold_in(keys[6], part), 71), part),
    }


epsilon = 1e-06

def label_max(scores, row_segments, flagged):
    block = math.gcd(LABELS, 8)

    def block_max(labels_block):
        member = row_segments[None, :] == labels_block[:, None]
        masked = jnp.where(member[:, :, None], scores[None, :, :], -jnp.inf)
        return lax.optimization_barrier(jnp.max(masked, axis=1))
    result = lax.map(block_max, flagged.reshape(LABELS // block, block))
    return result.reshape(LABELS, scores.shape[1])

def reference(queries, train_grads, precond, counts, segment_ids, flagged):
    query_full = queries.astype(jnp.float32)
    query_sq = lax.optimization_barrier(jnp.sum(query_full * query_full * precond[None, :], axis=1))
    normed = (query_full * precond[None, :] * lax.rsqrt(query_sq + epsilon)[:, None]).astype(jnp.bfloat16)

    def one_shard(inputs):
        shard_rows, live_count = inputs
        shard_full = shard_rows.astype(jnp.float32)
        train_sq = lax.optimization_barrier(jnp.sum(shard_full * shard_full * precond[None, :], axis=1))
        raw = lax.dot_general(normed, shard_rows, (((1,), (1,)), ((), ())), preferred_element_type=jnp.float32)
        scaled = raw * (math.sqrt(F) * lax.rsqrt(train_sq + epsilon))[None, :]
        pooled = label_max(scaled, segment_ids, flagged)
        live = jnp.arange(TDEV, dtype=jnp.int32) < live_count
        return jnp.where(live[:, None], pooled.T, jnp.float32(0.0))
    shards = train_grads.reshape(N_BLK, TDEV, F)
    result = lax.map(one_shard, (shards, counts))
    return result.reshape(NTRAIN, LABELS)
```

```python
import functools
import math

import jax
import jax.numpy as jnp
from jax import lax
from jax.experimental import pallas as pl
from jax.experimental.pallas import tpu as pltpu
from jax.sharding import PartitionSpec as P

F = 16384
epsilon = 1e-06
MESH = pl.DeviceIdType.MESH
f32 = jnp.float32


def iota(shape, dim):
    return lax.broadcasted_iota(jnp.int32, shape, dim)


def kernel(
    n, nf, C,
    q_hbm, t_hbm, p_ref, counts_ref, seg_ref, flagged_ref, flag_smem,
    out_ref,
    q_vmem, t_vmem, gath, onehot, segcol, acc, qacc, tacc, tsq, send, recv, pooled,
    q_sem, t_sem, zsend, zrecv, fsend, frecv,
):
    me = lax.axis_index("blk")
    myf = lax.axis_index("feat")
    rows = q_vmem.shape[0]
    half = rows // 2
    K = q_vmem.shape[1]
    kc = K // C
    T = t_vmem.shape[1]
    w = T // nf
    labels = flagged_ref.shape[1]

    barrier = pltpu.get_barrier_semaphore()

    @pl.when(me > 0)
    def _():
        pl.semaphore_signal(barrier, inc=1, device_id={"blk": me - 1}, device_id_type=MESH)

    @pl.when(me < n - 1)
    def _():
        pl.semaphore_signal(barrier, inc=1, device_id={"blk": me + 1}, device_id_type=MESH)

    for j in range(1, nf):
        pl.semaphore_signal(
            barrier, inc=1, device_id={"feat": lax.rem(myf + j, nf)}, device_id_type=MESH
        )

    q_copy = pltpu.make_async_copy(q_hbm, q_vmem, q_sem)
    q_copy.start()
    t_copies = []
    for c in range(C):
        t_copies.append(
            pltpu.make_async_copy(t_hbm.at[:, c * kc : (c + 1) * kc], t_vmem.at[c], t_sem.at[c])
        )
        t_copies[-1].start()

    flag_row = flagged_ref[...].astype(f32)
    eye = iota((labels, labels), 0) == iota((labels, labels), 1)
    flag_col = jnp.sum(jnp.where(eye, flag_row, 0.0), axis=1, keepdims=True)
    before = (iota((rows, rows), 0) < iota((rows, rows), 1)).astype(f32)
    for b in range(n):
        seg_row = seg_ref[:, b * rows : (b + 1) * rows].astype(f32)
        member = jnp.max(jnp.where(flag_col == seg_row, 1.0, 0.0), axis=0, keepdims=True)
        place = jnp.dot(
            jnp.broadcast_to(member, (8, rows)), before, preferred_element_type=f32
        )[0:1]
        slot = iota((half, rows), 0).astype(f32)
        hot = jnp.where((slot == place) & (member > 0.5), 1.0, 0.0)
        onehot[b] = hot
        ids = jnp.sum(hot * seg_row, axis=1, keepdims=True)
        segcol[b] = jnp.broadcast_to(ids, (half, w)).astype(jnp.int32)

    q_copy.wait()
    hot_me = onehot[me].astype(jnp.bfloat16)

    def zcopy(b, c, d):
        return pltpu.make_async_remote_copy(
            src_ref=gath.at[b, c],
            dst_ref=gath.at[b, c],
            send_sem=zsend.at[d, b, c],
            recv_sem=zrecv.at[b, c],
            device_id={"blk": me + (2 * d - 1)},
            device_id_type=MESH,
        )

    for c in range(C):
        picked = jnp.dot(
            hot_me, q_vmem[:, c * kc : (c + 1) * kc], preferred_element_type=f32
        )
        gath[me, c] = picked.astype(jnp.bfloat16)
        if c == 0:
            arrivals = (nf - 1) + jnp.where(me > 0, 1, 0) + jnp.where(me < n - 1, 1, 0)
            pl.semaphore_wait(barrier, arrivals)

        @pl.when(me > 0)
        def _():
            zcopy(me, c, 0).start()

        @pl.when(me < n - 1)
        def _():
            zcopy(me, c, 1).start()

    for t_copy in t_copies:
        t_copy.wait()

    def norm_rows(g, carry):
        base = pl.multiple_of(g * 32, 32)
        total = jnp.zeros((32, 128), f32)
        for c in range(C):
            for j in range(kc // 128):
                t = t_vmem[c, pl.ds(base, 32), j * 128 : (j + 1) * 128].astype(f32)
                at = c * kc + j * 128
                total = total + t * t * p_ref[:, at : at + 128]
        tacc[pl.ds(base, 32), :] = total
        return carry

    lax.fori_loop(0, T // 32, norm_rows, 0)
    for i in range(T // 128):
        turned = jnp.transpose(tacc[i * 128 : (i + 1) * 128, :])
        tsq[:, i * 128 : (i + 1) * 128] = jnp.sum(turned, axis=0, keepdims=True)

    def clear(d):
        acc[d] = jnp.zeros(acc.shape[1:], f32)
        qacc[d] = jnp.zeros(qacc.shape[1:], f32)

    def work(b, c, d):
        q = gath[b, c].astype(f32)
        x = q * p_ref[:, pl.ds(pl.multiple_of(c * kc, 128), kc)]
        hi = x.astype(jnp.bfloat16)
        lo = (x - hi.astype(f32)).astype(jnp.bfloat16)
        both = jnp.concatenate([hi, lo], axis=0)
        acc[d] += lax.dot_general(
            both, t_vmem[c], (((1,), (1,)), ((), ())), preferred_element_type=f32
        )
        sq = x * q
        total = qacc[d]
        for j in range(kc // 128):
            total = total + sq[:, j * 128 : (j + 1) * 128]
        qacc[d] = total

    def fcopy(b, f):
        return pltpu.make_async_remote_copy(
            src_ref=send.at[b, f],
            dst_ref=recv.at[b, myf],
            send_sem=fsend.at[b, f],
            recv_sem=frecv.at[b, myf],
            device_id={"feat": f},
            device_id_type=MESH,
        )

    def arrived(b, f):
        return pltpu.make_async_remote_copy(
            src_ref=recv.at[b, f],
            dst_ref=recv.at[b, f],
            send_sem=fsend.at[b, f],
            recv_sem=frecv.at[b, f],
            device_id={"feat": f},
            device_id_type=MESH,
        )

    diagonal = iota((half, w), 0) == iota((half, w), 1)

    def finish(b, d):
        s = acc[d, 0:half, :] + acc[d, half : 2 * half, :]
        q_col = jnp.sum(qacc[d], axis=1, keepdims=True)
        q_row = jnp.sum(jnp.where(diagonal, q_col, 0.0), axis=0, keepdims=True)
        t_row = tsq[...]
        line = iota((8, w), 0)
        for f in range(nf):
            cut = slice(f * w, (f + 1) * w)
            send[b, f, 0:half, :] = s[:, cut]
            send[b, f, half : half + 8, :] = jnp.where(
                line == 0, q_row, jnp.where(line == 1, t_row[:, cut], 0.0)
            )
        for j in range(1, nf):
            fcopy(b, lax.rem(myf + j, nf)).start()

    def collect(b):
        total = send[b, myf]
        for j in range(1, nf):
            f = lax.rem(myf + j, nf)
            arrived(b, f).wait_recv()
            total = total + recv[b, f]
        q_row = total[half : half + 1, :]
        q_col = jnp.sum(jnp.where(diagonal, q_row, 0.0), axis=1, keepdims=True)
        s = total[0:half, :] * lax.rsqrt(q_col + epsilon)
        ids = segcol[b]

        def one_label(l8, carry):
            base = pl.multiple_of(l8 * 8, 8)
            best = [
                jnp.max(jnp.where(ids == flag_smem[base + i], s, -jnp.inf), axis=0, keepdims=True)
                for i in range(8)
            ]
            best = jnp.concatenate(best, axis=0)
            pooled[pl.ds(base, 8), 0:w] = jnp.maximum(pooled[pl.ds(base, 8), 0:w], best)
            return carry

        lax.fori_loop(0, labels // 8, one_label, 0)
        return total[half + 1 : half + 2, :]

    pooled[...] = jnp.full(pooled.shape, -jnp.inf, f32)
    clear(0)

    def own(c, carry):
        work(me, c, 0)
        return carry

    lax.fori_loop(0, C, own, 0)
    finish(me, 0)

    def collect_step(s):
        @pl.when(me - s >= 0)
        def _():
            collect(me - s)

        @pl.when(me + s < n)
        def _():
            collect(me + s)

    def step(s, carry):
        low, high = me - s, me + s
        clear(0)
        clear(1)

        def chunk(c, inner):
            @pl.when(low >= 0)
            def _():
                zcopy(low, c, 1).wait_recv()

                @pl.when(me < n - 1)
                def _():
                    zcopy(low, c, 1).start()

            @pl.when(high < n)
            def _():
                zcopy(high, c, 0).wait_recv()

                @pl.when(me > 0)
                def _():
                    zcopy(high, c, 0).start()

            @pl.when(low >= 0)
            def _():
                work(low, c, 0)

            @pl.when(high < n)
            def _():
                work(high, c, 1)

            return inner

        lax.fori_loop(0, C, chunk, 0)

        @pl.when(low >= 0)
        def _():
            finish(low, 0)

        @pl.when(high < n)
        def _():
            finish(high, 1)

        @pl.when(s > 1)
        def _():
            collect_step(s - 1)

        return carry

    lax.fori_loop(1, n, step, 0)
    collect_step(n - 1)
    t_total = collect(me)

    scale = math.sqrt(F) * lax.rsqrt(t_total + epsilon)
    live = (myf * w + iota((1, w), 1)) < counts_ref[0]
    pooled[0:labels, 0:w] = jnp.where(live, pooled[0:labels, 0:w] * scale, 0.0)
    turned = jnp.transpose(pooled[...])
    out_ref[...] = turned[0:w, 0:labels]

    def drain_block(b, carry):
        for j in range(1, nf):
            fcopy(b, lax.rem(myf + j, nf)).wait_send()

        def drain_chunk(c, inner):
            @pl.when((me > 0) & (b >= me))
            def _():
                zcopy(b, c, 0).wait_send()

            @pl.when((me < n - 1) & (b <= me))
            def _():
                zcopy(b, c, 1).wait_send()

            return inner

        lax.fori_loop(0, C, drain_chunk, 0)
        return carry

    lax.fori_loop(0, n, drain_block, 0)


def per_device(n, nf, queries, train_grads, precond, counts, segment_ids, flagged):
    rows, K = queries.shape
    T = train_grads.shape[0]
    w = T // nf
    half = rows // 2
    labels = flagged.shape[0]
    C = 4
    kc = K // C
    vmem = pl.BlockSpec(memory_space=pltpu.VMEM)
    smem = pl.BlockSpec(memory_space=pltpu.SMEM)
    hbm = pl.BlockSpec(memory_space=pl.ANY)
    return pl.pallas_call(
        functools.partial(kernel, n, nf, C),
        out_shape=jax.ShapeDtypeStruct((w, labels), f32),
        in_specs=[hbm, hbm, vmem, smem, vmem, vmem, smem],
        out_specs=vmem,
        scratch_shapes=[
            pltpu.VMEM((rows, K), jnp.bfloat16),
            pltpu.VMEM((C, T, kc), jnp.bfloat16),
            pltpu.VMEM((n, C, half, kc), jnp.bfloat16),
            pltpu.VMEM((n, half, rows), f32),
            pltpu.VMEM((n, half, w), jnp.int32),
            pltpu.VMEM((2, 2 * half, T), f32),
            pltpu.VMEM((2, half, 128), f32),
            pltpu.VMEM((T, 128), f32),
            pltpu.VMEM((1, T), f32),
            pltpu.VMEM((n, nf, half + 8, w), f32),
            pltpu.VMEM((n, nf, half + 8, w), f32),
            pltpu.VMEM((128, 128), f32),
            pltpu.SemaphoreType.DMA,
            pltpu.SemaphoreType.DMA((C,)),
            pltpu.SemaphoreType.DMA((2, n, C)),
            pltpu.SemaphoreType.DMA((n, C)),
            pltpu.SemaphoreType.DMA((n, nf)),
            pltpu.SemaphoreType.DMA((n, nf)),
        ],
        compiler_params=pltpu.CompilerParams(
            collective_id=0, has_side_effects=True, vmem_limit_bytes=48 * 1024 * 1024
        ),
    )(
        queries,
        train_grads,
        precond.reshape(1, K),
        counts,
        segment_ids.reshape(1, -1),
        flagged.reshape(1, -1),
        flagged,
    )


def solution(mesh):
    return jax.shard_map(
        functools.partial(per_device, mesh.shape["blk"], mesh.shape["feat"]),
        mesh=mesh,
        in_specs=(
            P(("groups", "blk"), "feat"),
            P(("groups", "blk"), "feat"),
            P("feat"),
            P(("groups", "blk")),
            P("groups"),
            P("groups"),
        ),
        out_specs=P(("groups", "blk", "feat"), None),
        check_vma=False,
    )
```

```python
import functools
import math

import jax
import jax.numpy as jnp
from jax import lax
from jax.experimental import pallas as pl
from jax.experimental.pallas import tpu as pltpu
from jax.sharding import PartitionSpec as P

F = 16384
epsilon = 1e-06
MESH = pl.DeviceIdType.MESH
f32 = jnp.float32


def iota(shape, dim):
    return lax.broadcasted_iota(jnp.int32, shape, dim)


def kernel(
    n, nf, C,
    q_hbm, t_hbm, p_hbm, counts_hbm, seg_hbm, flagged_hbm,
    out_ref,
    p_ref, counts_ref, seg_ref, flagged_ref, flag_smem, small_sem,
    q_vmem, t_vmem, gath, onehot, segcol, acc, qacc, tacc, tsq, t_total, send, recv, pooled,
    q_sem, t_sem, zsend, zrecv, fsend, frecv,
):
    me = lax.axis_index("blk")
    myf = lax.axis_index("feat")
    rows = q_vmem.shape[0]
    half = rows // 2
    K = q_vmem.shape[1]
    kc = K // C
    T = t_vmem.shape[1]
    w = T // nf
    labels = flagged_ref.shape[1]

    barrier = pltpu.get_barrier_semaphore()

    @pl.when(me > 0)
    def _():
        pl.semaphore_signal(barrier, inc=1, device_id={"blk": me - 1}, device_id_type=MESH)

    @pl.when(me < n - 1)
    def _():
        pl.semaphore_signal(barrier, inc=1, device_id={"blk": me + 1}, device_id_type=MESH)

    for j in range(1, nf):
        pl.semaphore_signal(
            barrier, inc=1, device_id={"feat": lax.rem(myf + j, nf)}, device_id_type=MESH
        )

    small_copies = [
        pltpu.make_async_copy(src, dst, small_sem.at[i])
        for i, (src, dst) in enumerate(
            (
                (seg_hbm, seg_ref),
                (flagged_hbm, flagged_ref),
                (p_hbm, p_ref),
                (flagged_hbm, flag_smem),
                (counts_hbm, counts_ref),
            )
        )
    ]
    for small in small_copies[:2]:
        small.start()
    q_copy = pltpu.make_async_copy(q_hbm, q_vmem, q_sem)
    q_copy.start()
    t_copies = []
    for c in range(C):
        t_copies.append(
            pltpu.make_async_copy(t_hbm.at[:, c * kc : (c + 1) * kc], t_vmem.at[c], t_sem.at[c])
        )
        t_copies[-1].start()

    for small in small_copies[2:]:
        small.start()
    for small in small_copies[:2]:
        small.wait()

    flag_row = flagged_ref[...].astype(f32)
    eye = iota((labels, labels), 0) == iota((labels, labels), 1)
    flag_col = jnp.sum(jnp.where(eye, flag_row, 0.0), axis=1, keepdims=True)
    before = (iota((rows, rows), 0) < iota((rows, rows), 1)).astype(f32)
    for b in range(n):
        seg_row = seg_ref[:, b * rows : (b + 1) * rows].astype(f32)
        member = jnp.max(jnp.where(flag_col == seg_row, 1.0, 0.0), axis=0, keepdims=True)
        place = jnp.dot(
            jnp.broadcast_to(member, (8, rows)), before, preferred_element_type=f32
        )[0:1]
        slot = iota((half, rows), 0).astype(f32)
        hot = jnp.where((slot == place) & (member > 0.5), 1.0, 0.0)
        onehot[b] = hot
        ids = jnp.sum(hot * seg_row, axis=1, keepdims=True)
        segcol[b] = jnp.broadcast_to(ids, (half, w)).astype(jnp.int32)

    q_copy.wait()
    hot_me = onehot[me].astype(jnp.bfloat16)

    def zcopy(b, c, d):
        return pltpu.make_async_remote_copy(
            src_ref=gath.at[b, c],
            dst_ref=gath.at[b, c],
            send_sem=zsend.at[d, b, c],
            recv_sem=zrecv.at[b, c],
            device_id={"blk": me + (2 * d - 1)},
            device_id_type=MESH,
        )

    for c in range(C):
        picked = jnp.dot(
            hot_me, q_vmem[:, c * kc : (c + 1) * kc], preferred_element_type=f32
        )
        gath[me, c] = picked.astype(jnp.bfloat16)
        if c == 0:
            arrivals = (nf - 1) + jnp.where(me > 0, 1, 0) + jnp.where(me < n - 1, 1, 0)
            pl.semaphore_wait(barrier, arrivals)

        @pl.when(me > 0)
        def _():
            zcopy(me, c, 0).start()

        @pl.when(me < n - 1)
        def _():
            zcopy(me, c, 1).start()

    for waiting in small_copies[2:] + t_copies:
        waiting.wait()

    def norm_rows(g, carry):
        base = pl.multiple_of(g * 32, 32)
        total = jnp.zeros((32, 128), f32)
        for c in range(C):
            for j in range(kc // 128):
                t = t_vmem[c, pl.ds(base, 32), j * 128 : (j + 1) * 128].astype(f32)
                at = c * kc + j * 128
                total = total + t * t * p_ref[:, at : at + 128]
        tacc[pl.ds(base, 32), :] = total
        return carry

    lax.fori_loop(0, T // 32, norm_rows, 0)
    for i in range(T // 128):
        turned = jnp.transpose(tacc[i * 128 : (i + 1) * 128, :])
        tsq[:, i * 128 : (i + 1) * 128] = jnp.sum(turned, axis=0, keepdims=True)

    def clear(d):
        acc[d] = jnp.zeros(acc.shape[1:], f32)
        qacc[d] = jnp.zeros(qacc.shape[1:], f32)

    def work(b, c, d):
        q = gath[b, c].astype(f32)
        x = q * p_ref[:, pl.ds(pl.multiple_of(c * kc, 128), kc)]
        hi = x.astype(jnp.bfloat16)
        lo = (x - hi.astype(f32)).astype(jnp.bfloat16)
        both = jnp.concatenate([hi, lo], axis=0)
        acc[d] += lax.dot_general(
            both, t_vmem[c], (((1,), (1,)), ((), ())), preferred_element_type=f32
        )
        sq = x * q
        total = qacc[d]
        for j in range(kc // 128):
            total = total + sq[:, j * 128 : (j + 1) * 128]
        qacc[d] = total

    def fcopy(b, f):
        return pltpu.make_async_remote_copy(
            src_ref=send.at[b, f],
            dst_ref=recv.at[b, myf],
            send_sem=fsend.at[b, f],
            recv_sem=frecv.at[b, myf],
            device_id={"feat": f},
            device_id_type=MESH,
        )

    def arrived(b, f):
        return pltpu.make_async_remote_copy(
            src_ref=recv.at[b, f],
            dst_ref=recv.at[b, f],
            send_sem=fsend.at[b, f],
            recv_sem=frecv.at[b, f],
            device_id={"feat": f},
            device_id_type=MESH,
        )

    diagonal = iota((half, w), 0) == iota((half, w), 1)

    def finish(b, d):
        s = acc[d, 0:half, :] + acc[d, half : 2 * half, :]
        q_col = jnp.sum(qacc[d], axis=1, keepdims=True)
        q_row = jnp.sum(jnp.where(diagonal, q_col, 0.0), axis=0, keepdims=True)
        t_row = tsq[...]
        line = iota((8, w), 0)
        for f in range(nf):
            cut = slice(f * w, (f + 1) * w)
            send[b, f, 0:half, :] = s[:, cut]
            send[b, f, half : half + 8, :] = jnp.where(
                line == 0, q_row, jnp.where(line == 1, t_row[:, cut], 0.0)
            )
        for j in range(1, nf):
            fcopy(b, lax.rem(myf + j, nf)).start()

    def collect(b):
        total = send[b, myf]
        for j in range(1, nf):
            f = lax.rem(myf + j, nf)
            arrived(b, f).wait_recv()
            total = total + recv[b, f]
        q_row = total[half : half + 1, :]
        q_col = jnp.sum(jnp.where(diagonal, q_row, 0.0), axis=1, keepdims=True)
        s = total[0:half, :] * lax.rsqrt(q_col + epsilon)
        ids = segcol[b]

        def one_label(l8, carry):
            base = pl.multiple_of(l8 * 8, 8)
            best = [
                jnp.max(jnp.where(ids == flag_smem[0, base + i], s, -jnp.inf), axis=0, keepdims=True)
                for i in range(8)
            ]
            best = jnp.concatenate(best, axis=0)
            pooled[pl.ds(base, 8), :] = jnp.maximum(pooled[pl.ds(base, 8), :], best)
            return carry

        lax.fori_loop(0, labels // 8, one_label, 0)
        t_total[...] = total[half + 1 : half + 2, :]

    pooled[...] = jnp.full(pooled.shape, -jnp.inf, f32)
    clear(0)

    def own(c, carry):
        work(me, c, 0)
        return carry

    lax.fori_loop(0, C, own, 0)
    finish(me, 0)

    def collect_step(s):
        @pl.when(me - s >= 0)
        def _():
            collect(me - s)

        @pl.when(me + s < n)
        def _():
            collect(me + s)

    def step(s, carry):
        low, high = me - s, me + s
        clear(0)
        clear(1)

        def chunk(c, inner):
            @pl.when(low >= 0)
            def _():
                zcopy(low, c, 1).wait_recv()

                @pl.when(me < n - 1)
                def _():
                    zcopy(low, c, 1).start()

            @pl.when(high < n)
            def _():
                zcopy(high, c, 0).wait_recv()

                @pl.when(me > 0)
                def _():
                    zcopy(high, c, 0).start()

            @pl.when(low >= 0)
            def _():
                work(low, c, 0)

            @pl.when(high < n)
            def _():
                work(high, c, 1)

            return inner

        lax.fori_loop(0, C, chunk, 0)

        @pl.when(low >= 0)
        def _():
            finish(low, 0)

        @pl.when(high < n)
        def _():
            finish(high, 1)

        @pl.when(s == 1)
        def _():
            collect(me)

        @pl.when(s > 1)
        def _():
            collect_step(s - 1)

        return carry

    lax.fori_loop(1, n, step, 0)
    collect_step(n - 1)

    scale = math.sqrt(F) * lax.rsqrt(t_total[...] + epsilon)
    live = (myf * w + iota((1, w), 1)) < counts_ref[0]
    out_ref[...] = jnp.where(live, pooled[...] * scale, 0.0)

    def drain_block(b, carry):
        for j in range(1, nf):
            fcopy(b, lax.rem(myf + j, nf)).wait_send()

        def drain_chunk(c, inner):
            @pl.when((me > 0) & (b >= me))
            def _():
                zcopy(b, c, 0).wait_send()

            @pl.when((me < n - 1) & (b <= me))
            def _():
                zcopy(b, c, 1).wait_send()

            return inner

        lax.fori_loop(0, C, drain_chunk, 0)
        return carry

    lax.fori_loop(0, n, drain_block, 0)


def per_device(n, nf, queries, train_grads, precond, counts, segment_ids, flagged):
    rows, K = queries.shape
    T = train_grads.shape[0]
    w = T // nf
    half = rows // 2
    labels = flagged.shape[0]
    C = 4
    kc = K // C
    vmem = pl.BlockSpec(memory_space=pltpu.VMEM)
    hbm = pl.BlockSpec(memory_space=pltpu.HBM)
    pooled = pl.pallas_call(
        functools.partial(kernel, n, nf, C),
        out_shape=jax.ShapeDtypeStruct((labels, w), f32),
        in_specs=[hbm] * 6,
        out_specs=vmem,
        scratch_shapes=[
            pltpu.VMEM((1, K), f32),
            pltpu.SMEM((1,), jnp.int32),
            pltpu.VMEM((1, n * rows), jnp.int32),
            pltpu.VMEM((1, labels), jnp.int32),
            pltpu.SMEM((1, labels), jnp.int32),
            pltpu.SemaphoreType.DMA((5,)),
            pltpu.VMEM((rows, K), jnp.bfloat16),
            pltpu.VMEM((C, T, kc), jnp.bfloat16),
            pltpu.VMEM((n, C, half, kc), jnp.bfloat16),
            pltpu.VMEM((n, half, rows), f32),
            pltpu.VMEM((n, half, w), jnp.int32),
            pltpu.VMEM((2, 2 * half, T), f32),
            pltpu.VMEM((2, half, 128), f32),
            pltpu.VMEM((T, 128), f32),
            pltpu.VMEM((1, T), f32),
            pltpu.VMEM((1, w), f32),
            pltpu.VMEM((n, nf, half + 8, w), f32),
            pltpu.VMEM((n, nf, half + 8, w), f32),
            pltpu.VMEM((labels, w), f32),
            pltpu.SemaphoreType.DMA,
            pltpu.SemaphoreType.DMA((C,)),
            pltpu.SemaphoreType.DMA((2, n, C)),
            pltpu.SemaphoreType.DMA((n, C)),
            pltpu.SemaphoreType.DMA((n, nf)),
            pltpu.SemaphoreType.DMA((n, nf)),
        ],
        compiler_params=pltpu.CompilerParams(
            collective_id=0, has_side_effects=True, vmem_limit_bytes=63 * 1024 * 1024
        ),
    )(
        queries,
        train_grads,
        precond.reshape(1, K),
        counts,
        segment_ids.reshape(1, -1),
        flagged.reshape(1, -1),
    )
    return pooled.T


def solution(mesh):
    return jax.shard_map(
        functools.partial(per_device, mesh.shape["blk"], mesh.shape["feat"]),
        mesh=mesh,
        in_specs=(
            P(("groups", "blk"), "feat"),
            P(("groups", "blk"), "feat"),
            P("feat"),
            P(("groups", "blk")),
            P("groups"),
            P("groups"),
        ),
        out_specs=P(("groups", "blk", "feat"), None),
        check_vma=False,
    )
```

```python
import functools
import math

import jax
import jax.numpy as jnp
from jax import lax
from jax.experimental import pallas as pl
from jax.experimental.pallas import tpu as pltpu
from jax.sharding import PartitionSpec as P

F = 16384
epsilon = 1e-06
MESH = pl.DeviceIdType.MESH
f32 = jnp.float32


def iota(shape, dim):
    return lax.broadcasted_iota(jnp.int32, shape, dim)


def kernel(
    n, nf, C, pieces,
    q_hbm, t_hbm, p_hbm, counts_hbm, seg_hbm, flagged_hbm,
    out_ref,
    p_ref, counts_ref, seg_ref, flagged_ref, small_sem,
    q_vmem, t_vmem, gath, segcol, acc, qacc, tacc, tsq, t_total, send, recv, pooled, flagcol, scored,
    q_sem, t_sem, zsend, zrecv, fsend, frecv,
):
    me = lax.axis_index("blk")
    myf = lax.axis_index("feat")
    rows = q_vmem.shape[0]
    half = rows // 2
    K = q_vmem.shape[1]
    kc = K // C
    T = t_vmem.shape[1]
    w = T // nf
    labels = flagged_ref.shape[1]

    small_copies = [
        pltpu.make_async_copy(src, dst, small_sem.at[i])
        for i, (src, dst) in enumerate(
            (
                (seg_hbm, seg_ref),
                (flagged_hbm, flagged_ref),
                (p_hbm, p_ref),
                (counts_hbm, counts_ref),
            )
        )
    ]
    for small in small_copies[:2]:
        small.start()
    barrier = pltpu.get_barrier_semaphore()

    @pl.when(me > 0)
    def _():
        pl.semaphore_signal(barrier, inc=1, device_id={"blk": me - 1}, device_id_type=MESH)

    @pl.when(me < n - 1)
    def _():
        pl.semaphore_signal(barrier, inc=1, device_id={"blk": me + 1}, device_id_type=MESH)

    for j in range(1, nf):
        pl.semaphore_signal(
            barrier, inc=1, device_id={"feat": lax.rem(myf + j, nf)}, device_id_type=MESH
        )

    q_copy = pltpu.make_async_copy(q_hbm, q_vmem, q_sem)
    q_copy.start()
    t_copies = []
    for c in range(C):
        t_copies.append(
            pltpu.make_async_copy(t_hbm.at[:, c * kc : (c + 1) * kc], t_vmem.at[c], t_sem.at[c])
        )
        t_copies[-1].start()

    for small in small_copies[2:]:
        small.start()
    for small in small_copies[:2]:
        small.wait()

    flag_row = flagged_ref[...].astype(f32)
    eye = iota((labels, labels), 0) == iota((labels, labels), 1)
    flag_col = jnp.sum(jnp.where(eye, flag_row, 0.0), axis=1, keepdims=True)
    before = (iota((rows, rows), 0) < iota((rows, rows), 1)).astype(f32)
    slot = iota((half, rows), 0).astype(f32)

    def select(seg_row):
        member = jnp.max(jnp.where(flag_col == seg_row, 1.0, 0.0), axis=0, keepdims=True)
        place = jnp.dot(
            jnp.broadcast_to(member, (8, rows)), before, preferred_element_type=f32
        )[0:1]
        return jnp.where((slot == place) & (member > 0.5), 1.0, 0.0)

    seg_rows = [seg_ref[:, b * rows : (b + 1) * rows].astype(f32) for b in range(n)]
    seg_me = seg_rows[0]
    for b in range(1, n):
        seg_me = jnp.where(me == b, seg_rows[b], seg_me)
    hot_me = select(seg_me).astype(jnp.bfloat16)
    q_copy.wait()

    def zcopy(b, piece, d):
        cs = pl.ds(pieces[piece][0], pieces[piece][1])
        return pltpu.make_async_remote_copy(
            src_ref=gath.at[b, cs],
            dst_ref=gath.at[b, cs],
            send_sem=zsend.at[d, b, piece],
            recv_sem=zrecv.at[b, piece],
            device_id={"blk": me + (2 * d - 1)},
            device_id_type=MESH,
        )

    for i, (start, count) in enumerate(pieces):
        for c in range(start, start + count):
            picked = jnp.dot(
                hot_me, q_vmem[:, c * kc : (c + 1) * kc], preferred_element_type=f32
            )
            gath[me, c] = picked.astype(jnp.bfloat16)
        if i == 0:
            arrivals = (nf - 1) + jnp.where(me > 0, 1, 0) + jnp.where(me < n - 1, 1, 0)
            pl.semaphore_wait(barrier, arrivals)

        @pl.when(me > 0)
        def _():
            zcopy(me, i, 0).start()

        @pl.when(me < n - 1)
        def _():
            zcopy(me, i, 1).start()

    flagcol[...] = jnp.broadcast_to(flag_col, (labels, w))
    for b in range(n):
        ids = jnp.sum(select(seg_rows[b]) * seg_rows[b], axis=1, keepdims=True)
        segcol[b] = jnp.broadcast_to(ids, (half, w))

    for waiting in small_copies[2:] + t_copies:
        waiting.wait()

    def norm_rows(g, carry):
        base = pl.multiple_of(g * 32, 32)
        total = jnp.zeros((32, 128), f32)
        for c in range(C):
            for j in range(kc // 128):
                t = t_vmem[c, pl.ds(base, 32), j * 128 : (j + 1) * 128].astype(f32)
                at = c * kc + j * 128
                total = total + t * t * p_ref[:, at : at + 128]
        tacc[pl.ds(base, 32), :] = total
        return carry

    def norm_total():
        for i in range(T // 128):
            turned = jnp.transpose(tacc[i * 128 : (i + 1) * 128, :])
            tsq[:, i * 128 : (i + 1) * 128] = jnp.sum(turned, axis=0, keepdims=True)

    def clear(d):
        acc[d] = jnp.zeros(acc.shape[1:], f32)
        qacc[d] = jnp.zeros(qacc.shape[1:], f32)

    def work(b, c, d):
        q = gath[b, c].astype(f32)
        x = q * p_ref[:, pl.ds(pl.multiple_of(c * kc, 128), kc)]
        hi = x.astype(jnp.bfloat16)
        lo = (x - hi.astype(f32)).astype(jnp.bfloat16)
        both = jnp.concatenate([hi, lo], axis=0)
        acc[d] += lax.dot_general(
            both, t_vmem[c], (((1,), (1,)), ((), ())), preferred_element_type=f32
        )
        sq = x * q
        total = qacc[d]
        for j in range(kc // 128):
            total = total + sq[:, j * 128 : (j + 1) * 128]
        qacc[d] = total

    def fcopy(b, f):
        return pltpu.make_async_remote_copy(
            src_ref=send.at[b, f],
            dst_ref=recv.at[b, myf],
            send_sem=fsend.at[b, f],
            recv_sem=frecv.at[b, myf],
            device_id={"feat": f},
            device_id_type=MESH,
        )

    def arrived(b, f):
        return pltpu.make_async_remote_copy(
            src_ref=recv.at[b, f],
            dst_ref=recv.at[b, f],
            send_sem=fsend.at[b, f],
            recv_sem=frecv.at[b, f],
            device_id={"feat": f},
            device_id_type=MESH,
        )

    diagonal = iota((half, w), 0) == iota((half, w), 1)

    def finish(b, d):
        s = acc[d, 0:half, :] + acc[d, half : 2 * half, :]
        q_col = jnp.sum(qacc[d], axis=1, keepdims=True)
        q_row = jnp.sum(jnp.where(diagonal, q_col, 0.0), axis=0, keepdims=True)
        t_row = tsq[...]
        line = iota((8, w), 0)
        for f in range(nf):
            cut = slice(f * w, (f + 1) * w)
            send[b, f, 0:half, :] = s[:, cut]
            send[b, f, half : half + 8, :] = jnp.where(
                line == 0, q_row, jnp.where(line == 1, t_row[:, cut], 0.0)
            )
        for j in (*range(2, nf), 1):
            fcopy(b, lax.rem(myf + j, nf)).start()

    def collect(b):
        total = send[b, myf]
        for j in range(1, nf):
            f = lax.rem(myf + j, nf)
            arrived(b, f).wait_recv()
            total = total + recv[b, f]
        q_row = total[half : half + 1, :]
        q_col = jnp.sum(jnp.where(diagonal, q_row, 0.0), axis=1, keepdims=True)
        scored[...] = total[0:half, :] * lax.rsqrt(q_col + epsilon)
        names = flagcol[...]

        def some_rows(g, best):
            for i in range(8):
                r = pl.ds(g * 8 + i, 1)
                best = jnp.maximum(
                    best, jnp.where(names == segcol[b, r, :], scored[r, :], -jnp.inf)
                )
            return best

        pooled[...] = lax.fori_loop(0, half // 8, some_rows, pooled[...])
        t_total[...] = total[half + 1 : half + 2, :]

    pooled[...] = jnp.full(pooled.shape, -jnp.inf, f32)

    def collect_step(s):
        def side(d, carry):
            b = me + (2 * d - 1) * s

            @pl.when((b >= 0) & (b < n))
            def _():
                collect(b)

            return carry

        lax.fori_loop(0, 2, side, 0)

    def step(s, carry):
        low, high = me - s, me + s
        clear(0)
        clear(1)

        @pl.when(s == 1)
        def _():
            clear(2)

        for i, (start, count) in enumerate(pieces):
            @pl.when(low >= 0)
            def _():
                zcopy(low, i, 1).wait_recv()

                @pl.when(me < n - 1)
                def _():
                    zcopy(low, i, 1).start()

            @pl.when(high < n)
            def _():
                zcopy(high, i, 0).wait_recv()

                @pl.when(me > 0)
                def _():
                    zcopy(high, i, 0).start()

            def chunk(c, inner):
                @pl.when(s == 1)
                def _():
                    quarter = T // 32 // C
                    lax.fori_loop(c * quarter, (c + 1) * quarter, norm_rows, 0)
                    work(me, c, 2)

                @pl.when(low >= 0)
                def _():
                    work(low, c, 0)

                @pl.when(high < n)
                def _():
                    work(high, c, 1)

                return inner

            lax.fori_loop(start, start + count, chunk, 0)

            if i == max(len(pieces) - 2, 0):
                @pl.when(s == 2)
                def _():
                    collect(me)

                @pl.when(s > 1)
                def _():
                    collect_step(s - 1)

        @pl.when(s == 1)
        def _():
            norm_total()
            finish(me, 2)

        @pl.when(low >= 0)
        def _():
            finish(low, 0)

        @pl.when(high < n)
        def _():
            finish(high, 1)

        return carry

    lax.fori_loop(1, n, step, 0)
    if n == 2:
        collect(me)

    def drain_block(b, carry):
        for j in range(1, nf):
            fcopy(b, lax.rem(myf + j, nf)).wait_send()

        for i in range(len(pieces)):
            @pl.when((me > 0) & (b >= me))
            def _():
                zcopy(b, i, 0).wait_send()

            @pl.when((me < n - 1) & (b <= me))
            def _():
                zcopy(b, i, 1).wait_send()

        return carry

    lax.fori_loop(0, n, drain_block, 0)

    collect_step(n - 1)

    scale = math.sqrt(F) * lax.rsqrt(t_total[...] + epsilon)
    live = (myf * w + iota((1, w), 1)) < counts_ref[0]
    out_ref[...] = jnp.where(live, pooled[...] * scale, 0.0)


def per_device(n, nf, queries, train_grads, precond, counts, segment_ids, flagged):
    rows, K = queries.shape
    T = train_grads.shape[0]
    w = T // nf
    half = rows // 2
    labels = flagged.shape[0]
    C = 4
    pieces = ((0, 1), (1, 1), (2, 1), (3, 1))
    kc = K // C
    vmem = pl.BlockSpec(memory_space=pltpu.VMEM)
    hbm = pl.BlockSpec(memory_space=pltpu.HBM)
    pooled = pl.pallas_call(
        functools.partial(kernel, n, nf, C, pieces),
        out_shape=jax.ShapeDtypeStruct((labels, w), f32),
        in_specs=[hbm] * 6,
        out_specs=vmem,
        scratch_shapes=[
            pltpu.VMEM((1, K), f32),
            pltpu.SMEM((1,), jnp.int32),
            pltpu.VMEM((1, n * rows), jnp.int32),
            pltpu.VMEM((1, labels), jnp.int32),
            pltpu.SemaphoreType.DMA((4,)),
            pltpu.VMEM((rows, K), jnp.bfloat16),
            pltpu.VMEM((C, T, kc), jnp.bfloat16),
            pltpu.VMEM((n, C, half, kc), jnp.bfloat16),
            pltpu.VMEM((n, half, w), f32),
            pltpu.VMEM((3, 2 * half, T), f32),
            pltpu.VMEM((3, half, 128), f32),
            pltpu.VMEM((T, 128), f32),
            pltpu.VMEM((1, T), f32),
            pltpu.VMEM((1, w), f32),
            pltpu.VMEM((n, nf, half + 8, w), f32),
            pltpu.VMEM((n, nf, half + 8, w), f32),
            pltpu.VMEM((labels, w), f32),
            pltpu.VMEM((labels, w), f32),
            pltpu.VMEM((half, w), f32),
            pltpu.SemaphoreType.DMA,
            pltpu.SemaphoreType.DMA((C,)),
            pltpu.SemaphoreType.DMA((2, n, len(pieces))),
            pltpu.SemaphoreType.DMA((n, len(pieces))),
            pltpu.SemaphoreType.DMA((n, nf)),
            pltpu.SemaphoreType.DMA((n, nf)),
        ],
        compiler_params=pltpu.CompilerParams(
            collective_id=0, has_side_effects=True, vmem_limit_bytes=63 * 1024 * 1024
        ),
    )(
        queries,
        train_grads,
        precond.reshape(1, K),
        counts,
        segment_ids.reshape(1, -1),
        flagged.reshape(1, -1),
    )
    return pooled.T


def solution(mesh):
    return jax.shard_map(
        functools.partial(per_device, mesh.shape["blk"], mesh.shape["feat"]),
        mesh=mesh,
        in_specs=(
            P(("groups", "blk"), "feat"),
            P(("groups", "blk"), "feat"),
            P("feat"),
            P(("groups", "blk")),
            P("groups"),
            P("groups"),
        ),
        out_specs=P(("groups", "blk", "feat"), None),
        check_vma=False,
    )
```

```python
import functools
import math

import jax
import jax.numpy as jnp
from jax import lax
from jax.experimental import pallas as pl
from jax.experimental.pallas import tpu as pltpu
from jax.sharding import PartitionSpec as P

F = 16384
epsilon = 1e-06
MESH = pl.DeviceIdType.MESH
f32 = jnp.float32


def iota(shape, dim):
    return lax.broadcasted_iota(jnp.int32, shape, dim)


def kernel(
    n, nf, C, pieces,
    q_hbm, t_hbm, p_hbm, counts_hbm, seg_hbm, flagged_hbm,
    out_ref,
    p_ref, counts_ref, seg_ref, flagged_ref, small_sem,
    q_vmem, t_vmem, gath, segcol, acc, qacc, tacc, tsq, t_total, send, recv, pooled, flagcol, scored,
    q_sem, t_sem, zsend, zrecv, fsend, frecv,
):
    me = lax.axis_index("blk")
    myf = lax.axis_index("feat")
    rows = q_vmem.shape[0]
    half = rows // 2
    K = q_vmem.shape[1]
    kc = K // C
    T = t_vmem.shape[1]
    w = T // nf
    labels = flagged_ref.shape[1]

    small_copies = [
        pltpu.make_async_copy(src, dst, small_sem.at[i])
        for i, (src, dst) in enumerate(
            (
                (seg_hbm, seg_ref),
                (flagged_hbm, flagged_ref),
                (p_hbm, p_ref),
                (counts_hbm, counts_ref),
            )
        )
    ]
    for small in small_copies[:2]:
        small.start()
    barrier = pltpu.get_barrier_semaphore()

    @pl.when(me > 0)
    def _():
        pl.semaphore_signal(barrier, inc=1, device_id={"blk": me - 1}, device_id_type=MESH)

    @pl.when(me < n - 1)
    def _():
        pl.semaphore_signal(barrier, inc=1, device_id={"blk": me + 1}, device_id_type=MESH)

    for j in range(1, nf):
        pl.semaphore_signal(
            barrier, inc=1, device_id={"feat": lax.rem(myf + j, nf)}, device_id_type=MESH
        )

    q_copy = pltpu.make_async_copy(q_hbm, q_vmem, q_sem)
    q_copy.start()
    t_copies = []
    for c in range(C):
        t_copies.append(
            pltpu.make_async_copy(t_hbm.at[:, c * kc : (c + 1) * kc], t_vmem.at[c], t_sem.at[c])
        )
        t_copies[-1].start()

    for small in small_copies[2:]:
        small.start()
    for small in small_copies[:2]:
        small.wait()

    flag_row = flagged_ref[...].astype(f32)
    eye = iota((labels, labels), 0) == iota((labels, labels), 1)
    flag_col = jnp.sum(jnp.where(eye, flag_row, 0.0), axis=1, keepdims=True)
    before = (iota((rows, rows), 0) < iota((rows, rows), 1)).astype(f32)
    slot = iota((half, rows), 0).astype(f32)

    def select(seg_row):
        member = jnp.max(jnp.where(flag_col == seg_row, 1.0, 0.0), axis=0, keepdims=True)
        place = jnp.dot(
            jnp.broadcast_to(member, (8, rows)), before, preferred_element_type=f32
        )[0:1]
        return jnp.where((slot == place) & (member > 0.5), 1.0, 0.0)

    seg_rows = [seg_ref[:, b * rows : (b + 1) * rows].astype(f32) for b in range(n)]
    seg_me = seg_rows[0]
    for b in range(1, n):
        seg_me = jnp.where(me == b, seg_rows[b], seg_me)
    hot_me = select(seg_me).astype(jnp.bfloat16)
    q_copy.wait()

    def zcopy(b, piece, d):
        cs = pl.ds(pieces[piece][0], pieces[piece][1])
        return pltpu.make_async_remote_copy(
            src_ref=gath.at[b, cs],
            dst_ref=gath.at[b, cs],
            send_sem=zsend.at[d, b, piece],
            recv_sem=zrecv.at[b, piece],
            device_id={"blk": me + (2 * d - 1)},
            device_id_type=MESH,
        )

    for i, (start, count) in enumerate(pieces):
        for c in range(start, start + count):
            picked = jnp.dot(
                hot_me, q_vmem[:, c * kc : (c + 1) * kc], preferred_element_type=f32
            )
            gath[me, c] = picked.astype(jnp.bfloat16)
        if i == 0:
            arrivals = (nf - 1) + jnp.where(me > 0, 1, 0) + jnp.where(me < n - 1, 1, 0)
            pl.semaphore_wait(barrier, arrivals)

        @pl.when(me > 0)
        def _():
            zcopy(me, i, 0).start()

        @pl.when(me < n - 1)
        def _():
            zcopy(me, i, 1).start()

    flagcol[...] = jnp.broadcast_to(flag_col, (labels, w))
    for b in range(n):
        ids = jnp.sum(select(seg_rows[b]) * seg_rows[b], axis=1, keepdims=True)
        segcol[b] = jnp.broadcast_to(ids, (half, w))

    for waiting in small_copies[2:] + t_copies:
        waiting.wait()

    def norm_rows(g, carry):
        base = pl.multiple_of(g * 32, 32)
        total = jnp.zeros((32, 128), f32)
        for c in range(C):
            for j in range(kc // 128):
                t = t_vmem[c, pl.ds(base, 32), j * 128 : (j + 1) * 128].astype(f32)
                at = c * kc + j * 128
                total = total + t * t * p_ref[:, at : at + 128]
        tacc[pl.ds(base, 32), :] = total
        return carry

    def norm_total():
        for i in range(T // 128):
            turned = jnp.transpose(tacc[i * 128 : (i + 1) * 128, :])
            tsq[:, i * 128 : (i + 1) * 128] = jnp.sum(turned, axis=0, keepdims=True)

    def clear(d):
        acc[d] = jnp.zeros(acc.shape[1:], f32)
        qacc[d] = jnp.zeros(qacc.shape[1:], f32)

    def work(b, c, d):
        q = gath[b, c].astype(f32)
        x = q * p_ref[:, pl.ds(pl.multiple_of(c * kc, 128), kc)]
        hi = x.astype(jnp.bfloat16)
        lo = (x - hi.astype(f32)).astype(jnp.bfloat16)
        both = jnp.concatenate([hi, lo], axis=0)
        acc[d] += lax.dot_general(
            both, t_vmem[c], (((1,), (1,)), ((), ())), preferred_element_type=f32
        )
        sq = x * q
        total = qacc[d]
        for j in range(kc // 128):
            total = total + sq[:, j * 128 : (j + 1) * 128]
        qacc[d] = total

    def fcopy(b, f):
        return pltpu.make_async_remote_copy(
            src_ref=send.at[b, f],
            dst_ref=recv.at[b, myf],
            send_sem=fsend.at[b, f],
            recv_sem=frecv.at[b, myf],
            device_id={"feat": f},
            device_id_type=MESH,
        )

    def arrived(b, f):
        return pltpu.make_async_remote_copy(
            src_ref=recv.at[b, f],
            dst_ref=recv.at[b, f],
            send_sem=fsend.at[b, f],
            recv_sem=frecv.at[b, f],
            device_id={"feat": f},
            device_id_type=MESH,
        )

    diagonal = iota((half, w), 0) == iota((half, w), 1)

    def finish(b, d):
        s = acc[d, 0:half, :] + acc[d, half : 2 * half, :]
        q_col = jnp.sum(qacc[d], axis=1, keepdims=True)
        q_row = jnp.sum(jnp.where(diagonal, q_col, 0.0), axis=0, keepdims=True)
        t_row = tsq[...]
        line = iota((8, w), 0)
        for f in range(nf):
            cut = slice(f * w, (f + 1) * w)
            send[b, f, 0:half, :] = s[:, cut]
            send[b, f, half : half + 8, :] = jnp.where(
                line == 0, q_row, jnp.where(line == 1, t_row[:, cut], 0.0)
            )
        for j in (*range(2, nf), 1):
            fcopy(b, lax.rem(myf + j, nf)).start()

    def collect(b):
        total = send[b, myf]
        for j in range(1, nf):
            f = lax.rem(myf + j, nf)
            arrived(b, f).wait_recv()
            total = total + recv[b, f]
        q_row = total[half : half + 1, :]
        q_col = jnp.sum(jnp.where(diagonal, q_row, 0.0), axis=1, keepdims=True)
        scored[...] = total[0:half, :] * lax.rsqrt(q_col + epsilon)
        names = flagcol[...]

        def some_rows(g, best):
            for i in range(8):
                r = pl.ds(g * 8 + i, 1)
                best = jnp.maximum(
                    best, jnp.where(names == segcol[b, r, :], scored[r, :], -jnp.inf)
                )
            return best

        pooled[...] = lax.fori_loop(0, half // 8, some_rows, pooled[...])
        t_total[...] = total[half + 1 : half + 2, :]

    pooled[...] = jnp.full(pooled.shape, -jnp.inf, f32)

    def collect_step(s):
        def side(d, carry):
            b = me + (2 * d - 1) * s

            @pl.when((b >= 0) & (b < n))
            def _():
                collect(b)

            return carry

        lax.fori_loop(0, 2, side, 0)

    def step(s, carry):
        low, high = me - s, me + s
        clear(0)
        clear(1)

        @pl.when(s == 1)
        def _():
            clear(2)

        for i, (start, count) in enumerate(pieces):
            @pl.when(high < n)
            def _():
                zcopy(high, i, 0).wait_recv()

                @pl.when(me > 0)
                def _():
                    zcopy(high, i, 0).start()

            @pl.when(low >= 0)
            def _():
                zcopy(low, i, 1).wait_recv()

                @pl.when(me < n - 1)
                def _():
                    zcopy(low, i, 1).start()

            def chunk(c, inner):
                @pl.when(s == 1)
                def _():
                    quarter = T // 32 // C
                    lax.fori_loop(c * quarter, (c + 1) * quarter, norm_rows, 0)
                    work(me, c, 2)

                @pl.when(low >= 0)
                def _():
                    work(low, c, 0)

                @pl.when(high < n)
                def _():
                    work(high, c, 1)

                return inner

            lax.fori_loop(start, start + count, chunk, 0)

            if i == max(len(pieces) - 2, 0):
                @pl.when(s == 2)
                def _():
                    collect(me)

                @pl.when(s > 1)
                def _():
                    collect_step(s - 1)

        @pl.when(s == 1)
        def _():
            norm_total()
            finish(me, 2)

        @pl.when(low >= 0)
        def _():
            finish(low, 0)

        @pl.when(high < n)
        def _():
            finish(high, 1)

        return carry

    lax.fori_loop(1, n, step, 0)
    if n == 2:
        collect(me)

    def drain_block(b, carry):
        for j in range(1, nf):
            fcopy(b, lax.rem(myf + j, nf)).wait_send()

        for i in range(len(pieces)):
            @pl.when((me > 0) & (b >= me))
            def _():
                zcopy(b, i, 0).wait_send()

            @pl.when((me < n - 1) & (b <= me))
            def _():
                zcopy(b, i, 1).wait_send()

        return carry

    lax.fori_loop(0, n, drain_block, 0)

    collect_step(n - 1)

    scale = math.sqrt(F) * lax.rsqrt(t_total[...] + epsilon)
    live = (myf * w + iota((1, w), 1)) < counts_ref[0]
    out_ref[...] = jnp.where(live, pooled[...] * scale, 0.0)


def per_device(n, nf, queries, train_grads, precond, counts, segment_ids, flagged):
    rows, K = queries.shape
    T = train_grads.shape[0]
    w = T // nf
    half = rows // 2
    labels = flagged.shape[0]
    C = 4
    pieces = ((0, 1), (1, 1), (2, 1), (3, 1))
    kc = K // C
    vmem = pl.BlockSpec(memory_space=pltpu.VMEM)
    hbm = pl.BlockSpec(memory_space=pltpu.HBM)
    pooled = pl.pallas_call(
        functools.partial(kernel, n, nf, C, pieces),
        out_shape=jax.ShapeDtypeStruct((labels, w), f32),
        in_specs=[hbm] * 6,
        out_specs=vmem,
        scratch_shapes=[
            pltpu.VMEM((1, K), f32),
            pltpu.SMEM((1,), jnp.int32),
            pltpu.VMEM((1, n * rows), jnp.int32),
            pltpu.VMEM((1, labels), jnp.int32),
            pltpu.SemaphoreType.DMA((4,)),
            pltpu.VMEM((rows, K), jnp.bfloat16),
            pltpu.VMEM((C, T, kc), jnp.bfloat16),
            pltpu.VMEM((n, C, half, kc), jnp.bfloat16),
            pltpu.VMEM((n, half, w), f32),
            pltpu.VMEM((3, 2 * half, T), f32),
            pltpu.VMEM((3, half, 128), f32),
            pltpu.VMEM((T, 128), f32),
            pltpu.VMEM((1, T), f32),
            pltpu.VMEM((1, w), f32),
            pltpu.VMEM((n, nf, half + 8, w), f32),
            pltpu.VMEM((n, nf, half + 8, w), f32),
            pltpu.VMEM((labels, w), f32),
            pltpu.VMEM((labels, w), f32),
            pltpu.VMEM((half, w), f32),
            pltpu.SemaphoreType.DMA,
            pltpu.SemaphoreType.DMA((C,)),
            pltpu.SemaphoreType.DMA((2, n, len(pieces))),
            pltpu.SemaphoreType.DMA((n, len(pieces))),
            pltpu.SemaphoreType.DMA((n, nf)),
            pltpu.SemaphoreType.DMA((n, nf)),
        ],
        compiler_params=pltpu.CompilerParams(
            collective_id=0, has_side_effects=True, vmem_limit_bytes=63 * 1024 * 1024
        ),
    )(
        queries,
        train_grads,
        precond.reshape(1, K),
        counts,
        segment_ids.reshape(1, -1),
        flagged.reshape(1, -1),
    )
    return pooled.T


def solution(mesh):
    return jax.shard_map(
        functools.partial(per_device, mesh.shape["blk"], mesh.shape["feat"]),
        mesh=mesh,
        in_specs=(
            P(("groups", "blk"), "feat"),
            P(("groups", "blk"), "feat"),
            P("feat"),
            P(("groups", "blk")),
            P("groups"),
            P("groups"),
        ),
        out_specs=P(("groups", "blk", "feat"), None),
        check_vma=False,
    )
```
